32 devices in a mesh: gx: 8 (over y, x, core), gz: 4 (over z).
Axes of the slice: x: 2, y: 2, z: 4, core: 2. Of those that a mesh axis runs over, the one named last changes fastest.
Arguments:
- adjoint: float32 [3, 128, 128, 512], P(None, 'gx', None, 'gz'), may hold values from -6 to 6
- velocity: float32 [3, 128, 128, 512], P(None, 'gx', None, 'gz'), may hold values from -0.45 to 0.45
- viscosity: float32 [128, 128, 512], P('gx', None, 'gz'), may hold values from 0.02 to 0.15
- filters: bfloat16 [128, 512, 512], P(('gx', 'gz')), may hold values from -0.25 to 0.25
- block_tiles: int32 [128, 8], replicated, may hold values from 0 to 127, all different within a row
- tile_place: int32 [128], replicated, may hold values from 0 to 127, each once
Outputs:
- adjoint_out: float32 [3, 128, 128, 512], P(None, 'gx', None, 'gz')
- generator_tile_gradient: float32 [128, 3, 512], P(('gx', 'gz'))
The draws below stay inside these ranges and needn't reach their ends.
Inputs may be any that keep to these rules, and one draw needn't show every extreme that they name: `block_tiles`: each row lists 8 different tiles; every tile is listed by some block. `tile_place`: each tile exactly once.
All inputs are finite; a program needn't handle non-finite values.
Results may differ from the reference program's by a relative error of at most 0.0003.
Values sent between devices are 32-bit elements; how exact they have to be, the bound alone decides.
A program may use at most 192 MiB of HBM per device.

```python
import math
import jax
import jax.numpy as jnp
from jax import lax

BY = 4
BZ = 128
LIST = 8
BLK = 512
NB = 128
TILES = 128
NX = 128
NY = 128
NZ = 512
N_GZ = 4


def steps_of(rng, shape, shards, least, largest):
    factor_of, own = 1.0, jax.random.fold_in(rng, 6)
    for position, shards_of in shards:
        draws = jnp.exp(jax.random.uniform(jax.random.fold_in(own, position), (shards_of,), jnp.float32, least / len(shards), largest / len(shards)))
        factor_of = factor_of * jnp.repeat(draws, shape[position] // shards_of).reshape([-1 if axis == position else 1 for axis in range(len(shape))])
    return factor_of


def different_ones(rng, rows, amount, top, lift):
    sequence = jax.random.permutation(jax.random.fold_in(rng, 1), amount)
    favour = sequence
    for power in range(3):
        favour = favour * favour // amount
    favour = favour * lift // amount
    chance = jax.random.randint(jax.random.fold_in(rng, 2), (rows, amount), 0, 4096) + favour
    fixed_rows = jax.random.permutation(jax.random.fold_in(rng, 3), rows)[jnp.arange(amount) % rows]
    chance = jnp.where(jnp.arange(rows)[:, None] == fixed_rows[None, :], 1 << 14, chance)
    priority = chance * amount + jnp.arange(amount)
    return lax.top_k(priority.astype(jnp.int32), top)[1].astype(jnp.int32)


def normal_values(key, dims, spread, limit, cuts=(), dtype=jnp.bfloat16):
    level = steps_of(key, dims, cuts, -0.22, 0.18) if cuts else 1.0
    array = jax.random.normal(key, dims, jnp.float32) * spread * level
    return jnp.minimum(jnp.maximum(array, -limit), limit).astype(dtype)


def setup_inputs(seed: int = 0) -> dict:
    splits = jax.random.split(jax.random.key(seed), 7)
    return {
        "adjoint": normal_values(splits[0], (3, NX, NY, NZ), 1.0, 6.0, ((1, 8), (3, 4)), jnp.float32),
        "velocity": normal_values(splits[1], (3, NX, NY, NZ), 0.15, 0.45, ((1, 8), (3, 4)), jnp.float32),
        "viscosity": jnp.clip(jnp.exp(math.log(0.15) - 2.014903 * jax.random.uniform(splits[2], (NX, NY, NZ), jnp.float32) ** steps_of(splits[2], (NX, NY, NZ), ((0, 8), (2, 4)), -0.2, 0.2)), 0.02, 0.15),
        "filters": normal_values(splits[3], (TILES, BLK, BLK), BLK ** -0.5, 0.25, ((0, 32),)),
        "block_tiles": different_ones(splits[4], NB, TILES, LIST, 1024),
        "tile_place": jax.random.permutation(splits[5], TILES).astype(jnp.int32),
    }


def advance(padded, visc_pad, velocity):
    centre = padded[..., 1:-1, 1:-1, 1:-1]
    east_cell = padded[..., 2:, 1:-1, 1:-1]
    west_cell = padded[..., :-2, 1:-1, 1:-1]
    north_cell = padded[..., 1:-1, 2:, 1:-1]
    south_cell = padded[..., 1:-1, :-2, 1:-1]
    upper_cell = padded[..., 1:-1, 1:-1, 2:]
    lower_cell = padded[..., 1:-1, 1:-1, :-2]
    visc_mid = visc_pad[1:-1, 1:-1, 1:-1]
    east_face = 0.5 * (visc_mid + visc_pad[2:, 1:-1, 1:-1])
    west_face = 0.5 * (visc_mid + visc_pad[:-2, 1:-1, 1:-1])
    north_face = 0.5 * (visc_mid + visc_pad[1:-1, 2:, 1:-1])
    south_face = 0.5 * (visc_mid + visc_pad[1:-1, :-2, 1:-1])
    upper_face = 0.5 * (visc_mid + visc_pad[1:-1, 1:-1, 2:])
    lower_face = 0.5 * (visc_mid + visc_pad[1:-1, 1:-1, :-2])
    transport = 0.5 * (velocity[0] * (east_cell - west_cell) + velocity[1] * (north_cell - south_cell) + velocity[2] * (upper_cell - lower_cell))
    diffusion = east_face * (east_cell - centre) - west_face * (centre - west_cell)
    diffusion = diffusion + north_face * (north_cell - centre) - south_face * (centre - south_cell)
    diffusion = diffusion + upper_face * (upper_cell - centre) - lower_face * (centre - lower_cell)
    return centre + transport + diffusion


def pad_field(field):
    wrapped = jnp.pad(field, ((0, 0), (0, 0), (1, 1)), mode="wrap")
    return jnp.pad(wrapped, ((1, 1), (1, 1), (0, 0)))


def cut_blocks(face, group_list):
    comps, rows_all, cols_all = face.shape
    reshaped_array = face.reshape(comps, rows_all // BY, BY, group_list, cols_all // (group_list * BZ), BZ)
    return reshaped_array.transpose(3, 1, 4, 0, 2, 5).reshape(-1, comps * BY * BZ)


def reference(adjoint, velocity, viscosity, filters, block_tiles, tile_place):
    visc_pad = pad_field(viscosity)

    def two_steps(component):
        middle = advance(pad_field(component), visc_pad, velocity)
        return advance(pad_field(middle), visc_pad, velocity)

    adjoint_out = lax.map(two_steps, adjoint)
    face = adjoint_out[:, 0]
    blocks = cut_blocks(face, N_GZ)
    slots = tile_place[block_tiles].reshape(-1)
    sums = jnp.zeros((TILES, 3 * BLK), jnp.float32).at[slots].add(jnp.repeat(blocks, LIST, axis=0))
    tile_view = sums.reshape(TILES, 3, BLK)
    generator_tile_gradient = jnp.einsum("gvl,gls->gvs", tile_view, filters.astype(jnp.float32), precision=lax.Precision.HIGHEST)
    return adjoint_out, generator_tile_gradient
```

```python
import functools

import jax
import jax.numpy as jnp
from jax import lax
from jax.experimental import pallas as pl
from jax.experimental.pallas import tpu as pltpu
from jax.sharding import PartitionSpec as P

BY = 4
PAD = 8
MESH = pl.DeviceIdType.MESH


def split_parts(value):
    high = value.astype(jnp.bfloat16)
    low = (value - high.astype(jnp.float32)).astype(jnp.bfloat16)
    return high, low


def kernel(
    gxn, gzn, chunk,
    adj_hbm, vel_hbm, visc_hbm, filt_hbm, lists_ref, place_ref,
    out_hbm, grad_ref,
    lam, mid, visc, vel, filt, coef, out, pack, take, joined, gate, contrib, got, left_side,
    load_sem, store_sem, x_send, x_recv, z_send, z_recv, t_send, t_recv,
):
    comps, nx, ny, nz = adj_hbm.shape
    tiles = place_ref.shape[1]
    tile_rows = filt_hbm.shape[0]
    half = nx // 2
    gx = lax.axis_index("gx")
    gz = lax.axis_index("gz")
    upper = lax.rem(gz + 1, gzn)
    lower = lax.rem(gz + gzn - 1, gzn)
    me = gx * gzn + gz
    rows = pl.ds(PAD, ny)
    f32 = jnp.float32

    inner = pl.ds(1, nx)
    loads = [
        pltpu.make_async_copy(adj_hbm, lam.at[:, inner, rows, :], load_sem.at[0]),
        pltpu.make_async_copy(visc_hbm, visc.at[inner, rows, :], load_sem.at[1]),
        pltpu.make_async_copy(vel_hbm, vel, load_sem.at[2]),
        pltpu.make_async_copy(filt_hbm, filt, load_sem.at[3]),
    ]
    for load in loads:
        load.start()

    barrier = pltpu.get_barrier_semaphore()

    def greet(x, z):
        pl.semaphore_signal(barrier, inc=1, device_id=(x, z), device_id_type=MESH)

    greet(gx, upper)
    greet(gx, lower)

    @pl.when(gx < gxn - 1)
    def _():
        greet(gx + 1, gz)

    @pl.when(gx > 0)
    def _():
        greet(gx - 1, gz)

    for z in range(gzn):
        known = (z == gz) | (z == upper) | (z == lower)

        @pl.when(((gx == 0) & jnp.logical_not(known)) | ((gx == 1) & (z != gz)) | (gx > 1))
        def _():
            greet(0, z)

    @pl.when(gx == 0)
    def _():
        pl.semaphore_wait(barrier, gxn * gzn - 1)

    @pl.when((gx > 0) & (gx < gxn - 1))
    def _():
        pl.semaphore_wait(barrier, 4)

    @pl.when((gx > 0) & (gx == gxn - 1))
    def _():
        pl.semaphore_wait(barrier, 3)

    def layers(source, target, plane_dim, slot):
        def plane_of(ref, at, padded):
            index = (slice(None),) * plane_dim + (at,)
            return ref.at[index + ((rows, slice(None)) if padded else ())]

        down = pltpu.make_async_remote_copy(
            plane_of(source[0], source[1], source[3]), plane_of(target, nx + 1, True),
            x_send.at[slot], x_recv.at[slot], device_id=(gx - 1, gz), device_id_type=MESH)
        up = pltpu.make_async_remote_copy(
            plane_of(source[0], source[2], source[3]), plane_of(target, 0, True),
            x_send.at[slot + 1], x_recv.at[slot + 1], device_id=(gx + 1, gz), device_id_type=MESH)
        return down, up

    def start_layers(pair):
        @pl.when(gx > 0)
        def _():
            pair[0].start()

        @pl.when(gx < gxn - 1)
        def _():
            pair[1].start()

    def await_layers(pair):
        @pl.when(gx < gxn - 1)
        def _():
            pair[0].wait_recv()

        @pl.when(gx > 0)
        def _():
            pair[1].wait_recv()

    def await_sent(pair):
        @pl.when(gx > 0)
        def _():
            pair[0].wait_send()

        @pl.when(gx < gxn - 1)
        def _():
            pair[1].wait_send()

    visc_layers = layers((visc_hbm, 0, nx - 1, False), visc, 0, 0)
    lam_layers = layers((adj_hbm, 0, nx - 1, False), lam, 1, 2)
    mid_layers = layers((mid, 1, nx, True), mid, 1, 4)
    start_layers(visc_layers)
    start_layers(lam_layers)

    for ref in (lam, mid):
        ref[:, :, 0:PAD, :] = jnp.zeros((comps, nx + 2, PAD, nz), f32)
        ref[:, :, PAD + ny:, :] = jnp.zeros((comps, nx + 2, PAD, nz), f32)
    visc[:, 0:PAD, :] = jnp.zeros((nx + 2, PAD, nz), f32)
    visc[:, PAD + ny:, :] = jnp.zeros((nx + 2, PAD, nz), f32)
    pack[...] = jnp.zeros_like(pack)

    @pl.when(gx == 0)
    def _():
        lam[:, 0, rows, :] = jnp.zeros((comps, ny, nz), f32)
        mid[:, 0, rows, :] = jnp.zeros((comps, ny, nz), f32)
        visc[0, rows, :] = jnp.zeros((ny, nz), f32)

    @pl.when(gx == gxn - 1)
    def _():
        lam[:, nx + 1, rows, :] = jnp.zeros((comps, ny, nz), f32)
        mid[:, nx + 1, rows, :] = jnp.zeros((comps, ny, nz), f32)
        visc[nx + 1, rows, :] = jnp.zeros((ny, nz), f32)

    lane = lax.broadcasted_iota(jnp.int32, (chunk, nz), 1)
    pair_of = lax.rem(lane + 1, nz) // 2

    def columns(slot):
        to_upper = pltpu.make_async_remote_copy(
            pack.at[slot], take.at[slot, 0], z_send.at[2 * slot], z_recv.at[2 * slot],
            device_id=(gx, upper), device_id_type=MESH)
        to_lower = pltpu.make_async_remote_copy(
            pack.at[slot], take.at[slot, 1], z_send.at[2 * slot + 1], z_recv.at[2 * slot + 1],
            device_id=(gx, lower), device_id_type=MESH)
        return to_upper, to_lower

    def join(slot):
        for copy in columns(slot):
            copy.wait_recv()
        wide = lax.broadcasted_iota(jnp.int32, (ny, nz), 1)
        joined[slot] = jnp.where(lax.rem(wide, 2) == 0, take[slot, 1], take[slot, 0])

    def add_columns(slot, k, r, value):
        at = pl.ds(r, chunk)
        pack[slot, at, :] = jnp.where(pair_of == k, pltpu.roll(value, 2 * k, 1), pack[slot, at, :])

    def spanwise(slot, k, r, value):
        edge = pltpu.roll(joined[slot, pl.ds(r, chunk), :], lax.rem(nz - 2 * k, nz), 1)
        above = pltpu.roll(jnp.where(lane == 0, edge, value), nz - 1, 1)
        below = pltpu.roll(jnp.where(lane == nz - 1, edge, value), 1, 1)
        return above, below

    loads[0].wait()
    loads[1].wait()

    @pl.loop(0, nx)
    def _(x):
        for r in range(0, ny, chunk):
            at = pl.ds(PAD + r, chunk)
            for c in range(comps):
                add_columns(0, c * nx + x, r, lam[c, x + 1, at, :])
            add_columns(0, comps * nx + x, r, visc[x + 1, at, :])

    for copy in columns(0):
        copy.start()

    block_rows = ny // BY
    part = gate.shape[1]

    @pl.when(gx == 0)
    def _():
        lists = lists_ref[pl.ds(pl.multiple_of(gz * block_rows, block_rows), block_rows), :]
        tile_id = lax.broadcasted_iota(jnp.int32, (block_rows, tiles), 1)
        named = jnp.zeros((block_rows, tiles), f32)
        for l in range(lists.shape[1]):
            named = named + jnp.where(lists[:, l:l + 1] == tile_id, 1.0, 0.0)
        spread = (lax.broadcasted_iota(jnp.int32, (ny, block_rows), 0) // BY
                  == lax.broadcasted_iota(jnp.int32, (ny, block_rows), 1))
        named = jnp.dot(jnp.where(spread, 1.0, 0.0).astype(jnp.bfloat16), named.astype(jnp.bfloat16),
                        preferred_element_type=f32).astype(jnp.bfloat16)
        same_row = (lax.rem(lax.broadcasted_iota(jnp.int32, (part, ny), 0), BY)
                    == lax.rem(lax.broadcasted_iota(jnp.int32, (part, ny), 1), BY))

        @pl.loop(0, gate.shape[0])
        def _(j):
            wanted = (lax.broadcasted_iota(jnp.int32, (part, tiles), 0) + j * part) // BY
            moved = jnp.where(place_ref[...] == wanted, 1.0, 0.0).astype(jnp.bfloat16)
            chosen = lax.dot_general(moved, named, (((1,), (1,)), ((), ())), preferred_element_type=f32)
            gate[j] = jnp.where(same_row, chosen, 0.0).astype(jnp.bfloat16)

    loads[2].wait()
    await_layers(visc_layers)
    await_layers(lam_layers)
    join(0)

    def first_step(x, slot, k_of):
        for r in range(0, ny, chunk):
            at = pl.ds(PAD + r, chunk)
            plain = pl.ds(r, chunk)
            v = visc[x + 1, at, :]
            v_above, v_below = spanwise(0, comps * nx + x, r, v)
            faces = [0.5 * (v + other) for other in (
                visc[x + 2, at, :], visc[x, at, :],
                visc[x + 1, pl.ds(PAD + r + 1, chunk), :], visc[x + 1, pl.ds(PAD + r - 1, chunk), :],
                v_above, v_below)]
            total = ((faces[0] + faces[1]) + (faces[2] + faces[3])) + (faces[4] + faces[5])
            weights = []
            for d in range(3):
                speed = 0.5 * vel[d, x, plain, :]
                weights += [faces[2 * d] + speed, faces[2 * d + 1] - speed]
            weights.append(1.0 - total)
            for n, weight in enumerate(weights):
                coef[n, x, plain, :] = weight
            for c in range(comps):
                value = combine(lam, 0, c * nx + x, c, x, r, weights)
                mid[c, x + 1, at, :] = value
                add_columns(slot, k_of(c), r, value)

    def combine(field, slot, k, c, x, r, weights):
        at = pl.ds(PAD + r, chunk)
        centre = field[c, x + 1, at, :]
        above, below = spanwise(slot, k, r, centre)
        result = weights[6] * centre + weights[4] * above + weights[5] * below
        result = result + weights[0] * field[c, x + 2, at, :] + weights[1] * field[c, x, at, :]
        result = result + weights[2] * field[c, x + 1, pl.ds(PAD + r + 1, chunk), :]
        return result + weights[3] * field[c, x + 1, pl.ds(PAD + r - 1, chunk), :]

    first_step(0, 1, lambda c: c * half)
    first_step(nx - 1, 2, lambda c: c * half + half - 1)
    start_layers(mid_layers)

    @pl.loop(1, half)
    def _(x):
        first_step(x, 1, lambda c: c * half + x)

    for copy in columns(1):
        copy.start()

    @pl.loop(half, nx - 1)
    def _(x):
        first_step(x, 2, lambda c: c * half + x - half)

    for copy in columns(2):
        copy.start()

    def store(x):
        return pltpu.make_async_copy(out.at[:, x], out_hbm.at[:, x], store_sem.at[x])

    def second_step(x, slot, first):
        for r in range(0, ny, chunk):
            plain = pl.ds(r, chunk)
            weights = [coef[n, x, plain, :] for n in range(7)]
            for c in range(comps):
                out[c, x, plain, :] = combine(mid, slot, c * half + x - first, c, x, r, weights)
        store(x).start()

    join(1)
    await_layers(mid_layers)
    second_step(0, 1, 0)

    def tile_copy(d, source):
        return pltpu.make_async_remote_copy(
            contrib.at[d], got.at[source], t_send.at[d], t_recv.at[source],
            device_id=(d // gzn, lax.rem(d, gzn)), device_id_type=MESH)

    @pl.when(gx == 0)
    def _():
        owners = part // (tile_rows * BY)
        for c in range(comps):
            high, low = split_parts(out[c, 0])
            both = jnp.concatenate([high, low], axis=1)

            @pl.loop(0, gate.shape[0])
            def _(j):
                sums = jnp.dot(gate[j], both, preferred_element_type=f32)
                sums = sums[:, :nz] + sums[:, nz:]
                contrib[pl.ds(j * owners, owners), :, c * nz:(c + 1) * nz] = sums.reshape(
                    owners, tile_rows * BY, nz)

        got[gz] = contrib[me]

        @pl.loop(0, gxn * gzn)
        def _(d):
            @pl.when(d != me)
            def _():
                tile_copy(d, gz).start()

    @pl.loop(1, half)
    def _(x):
        second_step(x, 1, 0)

    join(2)

    @pl.loop(half, nx)
    def _(x):
        second_step(x, 2, half)

    for s in range(gzn):
        @pl.when((gx > 0) | (gz != s))
        def _():
            tile_copy(me, s).wait_recv()

    loads[3].wait()
    sums = got[0]
    for s in range(1, gzn):
        sums = sums + got[s]
    left_side[...] = jnp.zeros_like(left_side)
    for t in range(tile_rows):
        for c in range(comps):
            for i in range(BY):
                left_side[t, c:c + 1, i * nz:(i + 1) * nz] = sums[
                    t * BY + i:t * BY + i + 1, c * nz:(c + 1) * nz]
    for t in range(tile_rows):
        high, low = split_parts(left_side[t])
        product = (jnp.dot(high, filt[t], preferred_element_type=f32)
                   + jnp.dot(low, filt[t], preferred_element_type=f32))
        grad_ref[t] = product[:comps]

    for pair in (visc_layers, lam_layers, mid_layers):
        await_sent(pair)
    for slot in range(3):
        for copy in columns(slot):
            copy.wait_send()

    @pl.when(gx == 0)
    def _():
        @pl.loop(0, gxn * gzn)
        def _(d):
            @pl.when(d != me)
            def _():
                tile_copy(d, gz).wait_send()

    @pl.loop(0, nx)
    def _(x):
        store(x).wait()


def shards(adjoint, velocity, viscosity, filters, block_tiles, tile_place):
    gxn, gzn = lax.axis_size("gx"), lax.axis_size("gz")
    comps, nx, ny, nz = adjoint.shape
    tile_rows, order, _ = filters.shape
    tiles = tile_place.shape[0]
    devices = gxn * gzn
    part = min(512, tiles * BY)
    f32 = jnp.float32
    padded = (nx + 2, ny + 2 * PAD, nz)
    anywhere = pl.BlockSpec(memory_space=pl.ANY)
    vmem = pl.BlockSpec(memory_space=pltpu.VMEM)
    dma = pltpu.SemaphoreType.DMA
    return pl.pallas_call(
        functools.partial(kernel, gxn, gzn, 32),
        out_shape=(
            jax.ShapeDtypeStruct(adjoint.shape, f32),
            jax.ShapeDtypeStruct((tile_rows, comps, order), f32),
        ),
        in_specs=[anywhere] * 4 + [vmem] * 2,
        out_specs=(anywhere, vmem),
        scratch_shapes=[
            pltpu.VMEM((comps,) + padded, f32),
            pltpu.VMEM((comps,) + padded, f32),
            pltpu.VMEM(padded, f32),
            pltpu.VMEM(velocity.shape, f32),
            pltpu.VMEM(filters.shape, filters.dtype),
            pltpu.VMEM((7, nx, ny, nz), f32),
            pltpu.VMEM(adjoint.shape, f32),
            pltpu.VMEM((3, ny, nz), f32),
            pltpu.VMEM((3, 2, ny, nz), f32),
            pltpu.VMEM((3, ny, nz), f32),
            pltpu.VMEM((tiles * BY // part, part, ny), jnp.bfloat16),
            pltpu.VMEM((devices, tile_rows * BY, comps * nz), f32),
            pltpu.VMEM((gzn, tile_rows * BY, comps * nz), f32),
            pltpu.VMEM((tile_rows, 8, order), f32),
            dma((4,)),
            dma((nx,)),
            dma((6,)),
            dma((6,)),
            dma((6,)),
            dma((6,)),
            dma((devices,)),
            dma((gzn,)),
        ],
        compiler_params=pltpu.CompilerParams(
            collective_id=0, has_side_effects=True, vmem_limit_bytes=48 * 1024 * 1024
        ),
    )(adjoint, velocity, viscosity, filters, block_tiles, tile_place[None, :])


def solution(mesh):
    placed = (
        P(None, "gx", None, "gz"),
        P(None, "gx", None, "gz"),
        P("gx", None, "gz"),
        P(("gx", "gz"), None, None),
        P(),
        P(),
    )
    return jax.shard_map(
        shards,
        mesh=mesh,
        in_specs=placed,
        out_specs=(P(None, "gx", None, "gz"), P(("gx", "gz"), None, None)),
        check_vma=False,
    )
```

```python
import functools

import jax
import jax.numpy as jnp
from jax import lax
from jax.experimental import pallas as pl
from jax.experimental.pallas import tpu as pltpu
from jax.sharding import PartitionSpec as P

BY = 4
PAD = 8
MESH = pl.DeviceIdType.MESH


def split_parts(value):
    high = value.astype(jnp.bfloat16)
    low = (value - high.astype(jnp.float32)).astype(jnp.bfloat16)
    return high, low


def kernel(
    gxn, gzn, chunk,
    adj_hbm, vel_hbm, visc_hbm, filt_hbm, lists_ref, place_ref,
    out_hbm, grad_ref,
    lam, mid, visc, vel, filt, coef, out, pack, take, joined, gate, contrib, got, left_side,
    load_sem, store_sem, x_send, x_recv, z_send, z_recv, t_send, t_recv,
):
    comps, nx, ny, nz = adj_hbm.shape
    tiles = place_ref.shape[1]
    tile_rows = filt_hbm.shape[0]
    early = 3 * nx // 8
    face_at = nx // 2 + 1
    late = nx - early
    gx = lax.axis_index("gx")
    gz = lax.axis_index("gz")
    upper = lax.rem(gz + 1, gzn)
    lower = lax.rem(gz + gzn - 1, gzn)
    me = gx * gzn + gz
    rows = pl.ds(PAD, ny)
    f32 = jnp.float32

    inner = pl.ds(1, nx)
    loads = [
        pltpu.make_async_copy(adj_hbm, lam.at[:, inner, rows, :], load_sem.at[0]),
        pltpu.make_async_copy(visc_hbm, visc.at[inner, rows, :], load_sem.at[1]),
        pltpu.make_async_copy(vel_hbm, vel, load_sem.at[2]),
        pltpu.make_async_copy(filt_hbm, filt, load_sem.at[3]),
    ]
    for load in loads:
        load.start()

    barrier = pltpu.get_barrier_semaphore()

    def greet(x, z):
        pl.semaphore_signal(barrier, inc=1, device_id=(x, z), device_id_type=MESH)

    greet(gx, upper)
    greet(gx, lower)

    @pl.when(gx < gxn - 1)
    def _():
        greet(gx + 1, gz)

    @pl.when(gx > 0)
    def _():
        greet(gx - 1, gz)

    for z in range(gzn):
        known = (z == gz) | (z == upper) | (z == lower)

        @pl.when(((gx == 0) & jnp.logical_not(known)) | ((gx == 1) & (z != gz)) | (gx > 1))
        def _():
            greet(0, z)

    @pl.when(gx == 0)
    def _():
        pl.semaphore_wait(barrier, gxn * gzn - 1)

    @pl.when((gx > 0) & (gx < gxn - 1))
    def _():
        pl.semaphore_wait(barrier, 4)

    @pl.when((gx > 0) & (gx == gxn - 1))
    def _():
        pl.semaphore_wait(barrier, 3)

    def layers(source, target, plane_dim, slot):
        def plane_of(ref, at, padded):
            index = (slice(None),) * plane_dim + (at,)
            return ref.at[index + ((rows, slice(None)) if padded else ())]

        down = pltpu.make_async_remote_copy(
            plane_of(source[0], source[1], source[3]), plane_of(target, nx + 1, True),
            x_send.at[slot], x_recv.at[slot], device_id=(gx - 1, gz), device_id_type=MESH)
        up = pltpu.make_async_remote_copy(
            plane_of(source[0], source[2], source[3]), plane_of(target, 0, True),
            x_send.at[slot + 1], x_recv.at[slot + 1], device_id=(gx + 1, gz), device_id_type=MESH)
        return down, up

    def start_layers(pair):
        @pl.when(gx > 0)
        def _():
            pair[0].start()

        @pl.when(gx < gxn - 1)
        def _():
            pair[1].start()

    def await_layers(pair):
        @pl.when(gx < gxn - 1)
        def _():
            pair[0].wait_recv()

        @pl.when(gx > 0)
        def _():
            pair[1].wait_recv()

    def await_sent(pair):
        @pl.when(gx > 0)
        def _():
            pair[0].wait_send()

        @pl.when(gx < gxn - 1)
        def _():
            pair[1].wait_send()

    visc_layers = layers((visc_hbm, 0, nx - 1, False), visc, 0, 0)
    lam_layers = layers((adj_hbm, 0, nx - 1, False), lam, 1, 2)
    mid_layers = layers((mid, 1, nx, True), mid, 1, 4)
    start_layers(visc_layers)
    start_layers(lam_layers)

    for ref in (lam, mid):
        ref[:, :, 0:PAD, :] = jnp.zeros((comps, nx + 2, PAD, nz), f32)
        ref[:, :, PAD + ny:, :] = jnp.zeros((comps, nx + 2, PAD, nz), f32)
    visc[:, 0:PAD, :] = jnp.zeros((nx + 2, PAD, nz), f32)
    visc[:, PAD + ny:, :] = jnp.zeros((nx + 2, PAD, nz), f32)
    pack[...] = jnp.zeros_like(pack)

    @pl.when(gx == 0)
    def _():
        lam[:, 0, rows, :] = jnp.zeros((comps, ny, nz), f32)
        mid[:, 0, rows, :] = jnp.zeros((comps, ny, nz), f32)
        visc[0, rows, :] = jnp.zeros((ny, nz), f32)

    @pl.when(gx == gxn - 1)
    def _():
        lam[:, nx + 1, rows, :] = jnp.zeros((comps, ny, nz), f32)
        mid[:, nx + 1, rows, :] = jnp.zeros((comps, ny, nz), f32)
        visc[nx + 1, rows, :] = jnp.zeros((ny, nz), f32)

    lane = lax.broadcasted_iota(jnp.int32, (chunk, nz), 1)
    pair_of = lax.rem(lane + 1, nz) // 2

    def columns(slot):
        to_upper = pltpu.make_async_remote_copy(
            pack.at[slot], take.at[slot, 0], z_send.at[2 * slot], z_recv.at[2 * slot],
            device_id=(gx, upper), device_id_type=MESH)
        to_lower = pltpu.make_async_remote_copy(
            pack.at[slot], take.at[slot, 1], z_send.at[2 * slot + 1], z_recv.at[2 * slot + 1],
            device_id=(gx, lower), device_id_type=MESH)
        return to_upper, to_lower

    def join(slot):
        for copy in columns(slot):
            copy.wait_recv()
        wide = lax.broadcasted_iota(jnp.int32, (ny, nz), 1)
        joined[slot] = jnp.where(lax.rem(wide, 2) == 0, take[slot, 1], take[slot, 0])

    def add_columns(slot, k, r, value):
        at = pl.ds(r, chunk)
        pack[slot, at, :] = jnp.where(pair_of == k, pltpu.roll(value, 2 * k, 1), pack[slot, at, :])

    def spanwise(slot, k, r, value):
        edge = pltpu.roll(joined[slot, pl.ds(r, chunk), :], lax.rem(nz - 2 * k, nz), 1)
        above = pltpu.roll(jnp.where(lane == 0, edge, value), nz - 1, 1)
        below = pltpu.roll(jnp.where(lane == nz - 1, edge, value), 1, 1)
        return above, below

    loads[0].wait()
    loads[1].wait()

    @pl.loop(0, nx)
    def _(x):
        for r in range(0, ny, chunk):
            at = pl.ds(PAD + r, chunk)
            for c in range(comps):
                add_columns(0, c * nx + x, r, lam[c, x + 1, at, :])
            add_columns(0, comps * nx + x, r, visc[x + 1, at, :])

    for copy in columns(0):
        copy.start()

    block_rows = ny // BY
    part = gate.shape[1]

    @pl.when(gx == 0)
    def _():
        lists = lists_ref[pl.ds(pl.multiple_of(gz * block_rows, block_rows), block_rows), :]
        tile_id = lax.broadcasted_iota(jnp.int32, (block_rows, tiles), 1)
        named = jnp.zeros((block_rows, tiles), f32)
        for l in range(lists.shape[1]):
            named = named + jnp.where(lists[:, l:l + 1] == tile_id, 1.0, 0.0)
        spread = (lax.broadcasted_iota(jnp.int32, (ny, block_rows), 0) // BY
                  == lax.broadcasted_iota(jnp.int32, (ny, block_rows), 1))
        named = jnp.dot(jnp.where(spread, 1.0, 0.0).astype(jnp.bfloat16), named.astype(jnp.bfloat16),
                        preferred_element_type=f32).astype(jnp.bfloat16)
        same_row = (lax.rem(lax.broadcasted_iota(jnp.int32, (part, ny), 0), BY)
                    == lax.rem(lax.broadcasted_iota(jnp.int32, (part, ny), 1), BY))

        @pl.loop(0, gate.shape[0])
        def _(j):
            wanted = (lax.broadcasted_iota(jnp.int32, (part, tiles), 0) + j * part) // BY
            moved = jnp.where(place_ref[...] == wanted, 1.0, 0.0).astype(jnp.bfloat16)
            chosen = lax.dot_general(moved, named, (((1,), (1,)), ((), ())), preferred_element_type=f32)
            gate[j] = jnp.where(same_row, chosen, 0.0).astype(jnp.bfloat16)

    loads[2].wait()
    await_layers(visc_layers)
    await_layers(lam_layers)
    join(0)

    def first_step(x, slot, k_of):
        for r in range(0, ny, chunk):
            at = pl.ds(PAD + r, chunk)
            plain = pl.ds(r, chunk)
            v = visc[x + 1, at, :]
            v_above, v_below = spanwise(0, comps * nx + x, r, v)
            faces = [0.5 * (v + other) for other in (
                visc[x + 2, at, :], visc[x, at, :],
                visc[x + 1, pl.ds(PAD + r + 1, chunk), :], visc[x + 1, pl.ds(PAD + r - 1, chunk), :],
                v_above, v_below)]
            total = ((faces[0] + faces[1]) + (faces[2] + faces[3])) + (faces[4] + faces[5])
            weights = []
            for d in range(3):
                speed = 0.5 * vel[d, x, plain, :]
                weights += [faces[2 * d] + speed, faces[2 * d + 1] - speed]
            weights.append(1.0 - total)
            for n, weight in enumerate(weights):
                coef[n, x, plain, :] = weight
            for c in range(comps):
                value = combine(lam, 0, c * nx + x, c, x, r, weights)
                mid[c, x + 1, at, :] = value
                add_columns(slot, k_of(c), r, value)

    def combine(field, slot, k, c, x, r, weights):
        at = pl.ds(PAD + r, chunk)
        centre = field[c, x + 1, at, :]
        above, below = spanwise(slot, k, r, centre)
        result = weights[6] * centre + weights[4] * above + weights[5] * below
        result = result + weights[0] * field[c, x + 2, at, :] + weights[1] * field[c, x, at, :]
        result = result + weights[2] * field[c, x + 1, pl.ds(PAD + r + 1, chunk), :]
        return result + weights[3] * field[c, x + 1, pl.ds(PAD + r - 1, chunk), :]

    first_step(0, 1, lambda c: c * early)
    first_step(nx - 1, 2, lambda c: c * late + late - 1)
    start_layers(mid_layers)

    @pl.loop(1, early)
    def _(x):
        first_step(x, 1, lambda c: c * early + x)

    for copy in columns(1):
        copy.start()

    @pl.loop(early, face_at)
    def _(x):
        first_step(x, 2, lambda c: c * late + x - early)

    def store(x):
        return pltpu.make_async_copy(out.at[:, x], out_hbm.at[:, x], store_sem.at[x])

    def second_step(x, slot, first, count):
        for r in range(0, ny, chunk):
            plain = pl.ds(r, chunk)
            weights = [coef[n, x, plain, :] for n in range(7)]
            for c in range(comps):
                out[c, x, plain, :] = combine(mid, slot, c * count + x - first, c, x, r, weights)
        store(x).start()

    join(1)
    await_layers(mid_layers)
    second_step(0, 1, 0, early)

    def tile_copy(d, source):
        return pltpu.make_async_remote_copy(
            contrib.at[d], got.at[source], t_send.at[d], t_recv.at[source],
            device_id=(d // gzn, lax.rem(d, gzn)), device_id_type=MESH)

    @pl.when(gx == 0)
    def _():
        owners = part // (tile_rows * BY)
        for c in range(comps):
            high, low = split_parts(out[c, 0])
            both = jnp.concatenate([high, low], axis=1)

            @pl.loop(0, gate.shape[0])
            def _(j):
                sums = jnp.dot(gate[j], both, preferred_element_type=f32)
                sums = sums[:, :nz] + sums[:, nz:]
                contrib[pl.ds(j * owners, owners), :, c * nz:(c + 1) * nz] = sums.reshape(
                    owners, tile_rows * BY, nz)

        got[gz] = contrib[me]

        @pl.loop(0, gxn * gzn)
        def _(d):
            @pl.when(d != me)
            def _():
                tile_copy(d, gz).start()

    @pl.loop(face_at, nx - 1)
    def _(x):
        first_step(x, 2, lambda c: c * late + x - early)

    for copy in columns(2):
        copy.start()

    @pl.loop(1, early)
    def _(x):
        second_step(x, 1, 0, early)

    join(2)

    @pl.loop(early, nx)
    def _(x):
        second_step(x, 2, early, late)

    for s in range(gzn):
        @pl.when((gx > 0) | (gz != s))
        def _():
            tile_copy(me, s).wait_recv()

    loads[3].wait()
    sums = got[0]
    for s in range(1, gzn):
        sums = sums + got[s]
    left_side[...] = jnp.zeros_like(left_side)
    for t in range(tile_rows):
        for c in range(comps):
            for i in range(BY):
                left_side[t, c:c + 1, i * nz:(i + 1) * nz] = sums[
                    t * BY + i:t * BY + i + 1, c * nz:(c + 1) * nz]
    for t in range(tile_rows):
        high, low = split_parts(left_side[t])
        product = (jnp.dot(high, filt[t], preferred_element_type=f32)
                   + jnp.dot(low, filt[t], preferred_element_type=f32))
        grad_ref[t] = product[:comps]

    for pair in (visc_layers, lam_layers, mid_layers):
        await_sent(pair)
    for slot in range(3):
        for copy in columns(slot):
            copy.wait_send()

    @pl.when(gx == 0)
    def _():
        @pl.loop(0, gxn * gzn)
        def _(d):
            @pl.when(d != me)
            def _():
                tile_copy(d, gz).wait_send()

    @pl.loop(0, nx)
    def _(x):
        store(x).wait()


def move(source, target, sem):
    copies = [
        pltpu.make_async_copy(source.at[c, pl.ds(x, 4)], target.at[c, pl.ds(x, 4)], sem.at[c, x // 4])
        for c in range(source.shape[0]) for x in range(0, source.shape[1], 4)
    ]
    for copy in copies:
        copy.start()
    for copy in copies:
        copy.wait()


def shards(adjoint, velocity, viscosity, filters, block_tiles, tile_place):
    gxn, gzn = lax.axis_size("gx"), lax.axis_size("gz")
    comps, nx, ny, nz = adjoint.shape
    tile_rows, order, _ = filters.shape
    tiles = tile_place.shape[0]
    devices = gxn * gzn
    part = min(512, tiles * BY)
    f32 = jnp.float32
    padded = (nx + 2, ny + 2 * PAD, nz)
    anywhere = pl.BlockSpec(memory_space=pl.ANY)
    vmem = pl.BlockSpec(memory_space=pltpu.VMEM)
    dma = pltpu.SemaphoreType.DMA
    field, gradient = pl.pallas_call(
        functools.partial(kernel, gxn, gzn, 32),
        out_shape=(
            jax.ShapeDtypeStruct(adjoint.shape, f32),
            jax.ShapeDtypeStruct((tile_rows, comps, order), f32),
        ),
        in_specs=[anywhere] * 4 + [vmem] * 2,
        out_specs=(anywhere, vmem),
        scratch_shapes=[
            pltpu.VMEM((comps,) + padded, f32),
            pltpu.VMEM((comps,) + padded, f32),
            pltpu.VMEM(padded, f32),
            pltpu.VMEM(velocity.shape, f32),
            pltpu.VMEM(filters.shape, filters.dtype),
            pltpu.VMEM((7, nx, ny, nz), f32),
            pltpu.VMEM(adjoint.shape, f32),
            pltpu.VMEM((3, ny, nz), f32),
            pltpu.VMEM((3, 2, ny, nz), f32),
            pltpu.VMEM((3, ny, nz), f32),
            pltpu.VMEM((tiles * BY // part, part, ny), jnp.bfloat16),
            pltpu.VMEM((devices, tile_rows * BY, comps * nz), f32),
            pltpu.VMEM((gzn, tile_rows * BY, comps * nz), f32),
            pltpu.VMEM((tile_rows, 8, order), f32),
            dma((4,)),
            dma((nx,)),
            dma((6,)),
            dma((6,)),
            dma((6,)),
            dma((6,)),
            dma((devices,)),
            dma((gzn,)),
        ],
        compiler_params=pltpu.CompilerParams(
            collective_id=0, has_side_effects=True, vmem_limit_bytes=62 * 1024 * 1024
        ),
    )(adjoint, velocity, viscosity, filters, block_tiles, tile_place[None, :])
    field = pl.pallas_call(
        move,
        out_shape=jax.ShapeDtypeStruct(field.shape, f32),
        in_specs=[anywhere],
        out_specs=anywhere,
        scratch_shapes=[dma((comps, nx // 4))],
        compiler_params=pltpu.CompilerParams(vmem_limit_bytes=62 * 1024 * 1024),
    )(field)
    return field, gradient


def solution(mesh):
    placed = (
        P(None, "gx", None, "gz"),
        P(None, "gx", None, "gz"),
        P("gx", None, "gz"),
        P(("gx", "gz"), None, None),
        P(),
        P(),
    )
    return jax.shard_map(
        shards,
        mesh=mesh,
        in_specs=placed,
        out_specs=(P(None, "gx", None, "gz"), P(("gx", "gz"), None, None)),
        check_vma=False,
    )
```
